32 devices in a mesh: visit: 4 (over y, x), raft: 8 (over z, core).
Axes of the slice: x: 2, y: 2, z: 4, core: 2. Of those that a mesh axis runs over, the one named last changes fastest.
Arguments:
- tiles: bfloat16 [3072, 16384], P(('visit', 'raft')), may hold values from -6 to 6
- weights: float32 [3072], P(('visit', 'raft')), may hold values from 0.25 to 4
- coef: float32 [3072, 27], P(('visit', 'raft')), may hold values from -4 to 4
- owner: int32 [3072, 1], P(('visit', 'raft')), may hold values from 0 to 7; in each aligned block of 96 rows (0 to 95, 96 to 191, ...) at most 24 rows name the same one
- patch: int32 [3072], P(('visit', 'raft')), may hold values from 0 to 23
- row_taps: bfloat16 [27, 41], replicated, may hold values from -1 to 1
- col_taps: bfloat16 [27, 41], replicated, may hold values from -1 to 1
Outputs:
- coadd_image: float32 [8, 24, 128, 128], P('raft', 'visit')
The draws below stay inside these ranges and needn't reach their ends.
Inputs may be any that keep to these rules, and one draw needn't show every extreme that they name: Among the 96 tiles of one device (aligned blocks of rows in order), at most 24 name the same owner; in some blocks one owner is named by exactly 24.
All inputs are finite; a program needn't handle non-finite values.
Results may differ from the reference program's by a relative error of at most 0.0052.
Values may be sent and summed in bfloat16 or wider, within the bound.
A program may use at most 192 MiB of HBM per device.

```python
import math
import jax
import jax.numpy as jnp
import numpy as np
from jax import lax

SIDE = 128
KERNEL = 41
NB = 27
TILES_DEV = 96
PATCH_DEV = 24
MOST = 24
TILES = 3072
PIXELS = 16384
N_VISIT = 4
N_RAFT = 8


def set_ends(values, stream_key, low, top_value):
    longest = values.shape.index(max(values.shape))
    spots = []
    for shift in (0, 1):
        where = [jax.random.randint(jax.random.fold_in(stream_key, axis), (), 0, length) for axis, length in enumerate(values.shape)]
        where[longest] = (where[longest] + shift) % values.shape[longest]
        spots.append(tuple(where))
    return values.at[spots[0]].set(low).at[spots[1]].set(top_value)


def levels(stream_key, extent, shards, least, high):
    factor_of, own = 1.0, jax.random.fold_in(stream_key, 6)
    for position, shards_of in shards:
        steps = jnp.exp(jax.random.uniform(jax.random.fold_in(own, position), (shards_of,), jnp.float32, least / len(shards), high / len(shards)))
        factor_of = factor_of * jnp.repeat(steps, extent[position] // shards_of).reshape([-1 if axis == position else 1 for axis in range(len(extent))])
    return factor_of


def shared_out(key, own, number, rows, count, top, limit, slope):
    order = jax.random.permutation(key, count)
    crowded, ordinary = shares(count, rows * top, limit, slope, True), shares(count, rows * top, limit, slope, False)
    places = jnp.arange(count)

    def named(sizes, rotation):
        used = int((sizes > 0).sum())
        fixed = max(1, used // 4)
        passed = fixed + (places - fixed + rotation * (used - fixed)) % max(1, count - fixed)
        return jnp.zeros((count,), jnp.int32).at[order[jnp.where(places < fixed, places, passed)]].set(jnp.asarray(sizes, jnp.int32))

    sizes = jnp.where(number % 4 == 0, named(crowded, number // 4), named(ordinary, number - number // 4 - 1))
    mixed = jax.random.permutation(jax.random.fold_in(own, 3), count)
    donor, taker = mixed[0:count // 2 * 2:2], mixed[1:count // 2 * 2:2]
    slack = jnp.minimum(sizes[donor] - 1, limit - sizes[taker]) // 2
    slack = jnp.where((donor == order[0]) | (taker == order[0]) | (sizes[taker] == 0), 0, jnp.maximum(slack, 0))
    passed = jax.random.randint(jax.random.fold_in(own, 4), (count // 2,), 0, 1 << 20) % (slack + 1)
    sizes = sizes.at[donor].add(-passed).at[taker].add(passed)
    labels = jnp.searchsorted(jnp.cumsum(sizes), jnp.arange(rows * top), side="right").astype(jnp.int32)
    grid = labels.reshape(top, rows).T
    grid = grid[jax.random.permutation(jax.random.fold_in(own, 1), rows)]
    rotation = jax.random.randint(jax.random.fold_in(own, 2), (rows, 1), 0, top)
    return jnp.take_along_axis(grid, (jnp.arange(top)[None, :] + rotation) % top, axis=1)


def shares(count, total, reach, slope, full):
    weights = [(1 << 20) // math.isqrt(rank ** slope) + 1 for rank in range(1, count + 1)]
    largest = reach if full else min(reach, max(-(-total // count), total * weights[0] // sum(weights)))
    least = 1 if total - largest >= count - 1 else 0
    counts, surplus = [largest] + [least] * (count - 1), total - largest - least * (count - 1)
    while surplus > 0:
        candidates = [i for i in range(1, count) if counts[i] < largest] or [i for i in range(1, count) if counts[i] < reach]
        whole, left = sum([weights[i] for i in candidates]), surplus
        for i in candidates:
            more = min(reach - counts[i], max(1, left * weights[i] // whole), surplus)
            counts[i] = counts[i] + more
            surplus = surplus - more
    return np.array(counts)


def bell_draw(stream_key, shape, scale, bound, split=(), held_as=jnp.bfloat16):
    entries = scale * jax.random.normal(stream_key, shape, jnp.float32)
    if split:
        entries = entries * levels(stream_key, shape, split, -0.22, 0.18)
    return jnp.clip(entries, -bound, bound).astype(held_as)


def setup_inputs(seed: int = 0) -> dict:
    seeds = jax.random.split(jax.random.key(seed), 8)
    tiles = bell_draw(seeds[0], (TILES, PIXELS), 1.0, 6.0, ((0, 32),))
    weights = jnp.clip(jnp.exp(math.log(4.0) - 2.7725887 * jax.random.uniform(seeds[1], (TILES,), jnp.float32) ** levels(seeds[1], (TILES,), ((0, 32),), -0.2, 0.2)), 0.25, 4.0)
    coef = bell_draw(seeds[2], (TILES, NB), 1.0, 4.0, ((0, 32),), jnp.float32)
    owner_keys = jax.random.split(jax.random.fold_in(seeds[3], 1), TILES // TILES_DEV)
    owner_turns = jax.random.permutation(jax.random.fold_in(seeds[3], 3), TILES // TILES_DEV)
    owner = jax.vmap(lambda own, number: shared_out(jax.random.fold_in(seeds[3], 2), own, number, TILES_DEV, N_RAFT, 1, MOST, 2))(owner_keys, owner_turns).reshape((TILES, 1))
    patch = set_ends(jax.random.randint(seeds[4], (TILES,), 0, PATCH_DEV), jax.random.fold_in(seeds[4], 1), 0, PATCH_DEV - 1).astype(jnp.int32)
    row_taps = bell_draw(seeds[5], (NB, KERNEL), KERNEL ** -0.5, 1.0)
    col_taps = bell_draw(seeds[6], (NB, KERNEL), KERNEL ** -0.5, 1.0)
    return {"tiles": tiles, "weights": weights, "coef": coef, "owner": owner, "patch": patch, "row_taps": row_taps, "col_taps": col_taps}


def rounded(values):
    return lax.optimization_barrier(values.astype(jnp.bfloat16)).astype(jnp.float32)


def reference(tiles, weights, coef, owner, patch, row_taps, col_taps):
    half_width = (KERNEL - 1) // 2
    segment_total = N_RAFT * PATCH_DEV
    keys_all = (owner[:, 0] * PATCH_DEV + patch).astype(jnp.int32)
    scaled = rounded(weights[:, None] * coef)
    plain_weight = rounded(weights)
    weight_total = jax.ops.segment_sum(plain_weight, keys_all, num_segments=segment_total)
    numerator = jnp.zeros((N_RAFT * SIDE, PATCH_DEV * SIDE), jnp.float32)
    group_len = TILES_DEV * N_RAFT
    row_values = row_taps.astype(jnp.float32)
    col_values = col_taps.astype(jnp.float32)
    for group in range(N_VISIT):
        start = group * group_len
        group_keys = keys_all[start:start + group_len]
        order = jnp.argsort(group_keys, stable=True)
        sorted_keys = group_keys[order]
        sorted_tiles = tiles[start:start + group_len][order].astype(jnp.float32)
        sorted_scale = scaled[start:start + group_len][order]

        def basis_step(total, items):
            scale_column, row_tap, col_tap = items
            plane = jax.ops.segment_sum(sorted_tiles * scale_column[:, None], sorted_keys,
                                        num_segments=segment_total, indices_are_sorted=True)
            plane = rounded(plane)
            image = plane.reshape(N_RAFT, PATCH_DEV, SIDE, SIDE).transpose(0, 2, 1, 3)
            image = image.reshape(N_RAFT * SIDE, PATCH_DEV * SIDE)
            filtered = lax.conv_general_dilated(image[None, None], col_tap[None, None, None, :], (1, 1),
                                                ((0, 0), (half_width, half_width)),
                                                precision=lax.Precision.HIGHEST)[0, 0]
            filtered = rounded(filtered)
            result = lax.conv_general_dilated(filtered[None, None], row_tap[None, None, :, None], (1, 1),
                                              ((half_width, half_width), (0, 0)),
                                              precision=lax.Precision.HIGHEST)[0, 0]
            return total + result, None

        numerator, _ = lax.scan(basis_step, numerator, (sorted_scale.T, row_values, col_values))
    arranged = numerator.reshape(N_RAFT, SIDE, PATCH_DEV, SIDE).transpose(0, 2, 1, 3)
    return arranged / (1.0 + weight_total.reshape(N_RAFT, PATCH_DEV))[:, :, None, None]
```

```python
import functools

import jax
import jax.numpy as jnp
from jax import lax
from jax.experimental import pallas as pl
from jax.experimental.pallas import tpu as pltpu
from jax.sharding import Mesh, PartitionSpec as P

SIDE = 128
KERNEL = 41
NB = 27
PATCH_DEV = 24
GROUP = 9
HALF = (KERNEL - 1) // 2
TOP = 24
OUT_ROWS = 176


def with_halo(shard, sides, width):
    for axis, dim in sides:
        size, length = (lax.axis_size(axis), shard.shape[dim])
        up = [(i, (i + 1) % size) for i in range(size - 1)]
        down = [(j, i) for i, j in up]
        last = lax.slice_in_dim(shard, length - width, length, axis=dim)
        leading = lax.slice_in_dim(shard, 0, width, axis=dim)
        before = lax.ppermute(last, axis, up)
        after = lax.ppermute(leading, axis, down)
        shard = jnp.concatenate([before, shard, after], axis=dim)
    return shard


def tap_band(tap_values, offsets):
    selector = (offsets[:, :, None] == jnp.arange(tap_values.shape[1])[None, None, :]).astype(
        jnp.float32
    )
    return jnp.einsum("qrj,bj->bqr", selector, tap_values.astype(jnp.float32)).astype(jnp.bfloat16)


def body(tiles, weights, coef, owner, patch, row_taps, col_taps):
    tile_count = tiles.shape[0]
    peer_count = lax.axis_size("raft")
    capacity = max(2, 2 * tile_count // peer_count)
    half_width = (KERNEL - 1) // 2
    owner_ids = owner[:, 0]
    owner_hits = (owner_ids[:, None] == jnp.arange(peer_count)[None, :]).astype(jnp.int32)
    slot_rank = jnp.sum(jnp.cumsum(owner_hits, axis=0) * owner_hits, axis=1) - 1
    slot_index = owner_ids * capacity + slot_rank
    placing = (jnp.arange(peer_count * capacity)[:, None] == slot_index[None, :]).astype(
        jnp.bfloat16
    )
    scaled = (weights[:, None] * coef).astype(jnp.bfloat16)
    plain_weight = weights.astype(jnp.bfloat16)[:, None]
    tile_terms = jnp.concatenate([scaled, plain_weight], axis=1)
    patch_hits = (patch[:, None] == jnp.arange(PATCH_DEV)[None, :]).astype(jnp.bfloat16)
    mixing = (tile_terms[:, :, None] * patch_hits[:, None, :]).reshape(
        tile_count, (NB + 1) * PATCH_DEV
    )
    send_tiles = jnp.dot(placing, tiles, preferred_element_type=jnp.float32).astype(jnp.bfloat16)
    send_mixing = jnp.dot(placing, mixing, preferred_element_type=jnp.float32).astype(jnp.bfloat16)
    got_tiles, got_mixing = (
        lax.all_to_all(send_tiles, "raft", split_axis=0, concat_axis=0, tiled=True),
        lax.all_to_all(send_mixing, "raft", split_axis=0, concat_axis=0, tiled=True),
    )
    planes = lax.dot_general(
        got_mixing[:, : NB * PATCH_DEV],
        got_tiles,
        (((0,), (0,)), ((), ())),
        preferred_element_type=jnp.float32,
    )
    planes = planes.astype(jnp.bfloat16).reshape(NB, PATCH_DEV, SIDE, SIDE)
    weight_sum = jnp.sum(got_mixing[:, NB * PATCH_DEV :].astype(jnp.float32), axis=0)
    blank_rim = jnp.zeros((NB, 1, SIDE, half_width), jnp.bfloat16)
    left_rim = jnp.concatenate([blank_rim, planes[:, :-1, :, SIDE - half_width :]], axis=1)
    right_rim = jnp.concatenate([planes[:, 1:, :, :half_width], blank_rim], axis=1)
    window = jnp.concatenate([left_rim, planes, right_rim], axis=3)
    wide_index = jnp.arange(SIDE + 2 * half_width)
    narrow = jnp.arange(SIDE)
    col_band = tap_band(col_taps, wide_index[:, None] - narrow[None, :])
    filtered = jnp.einsum(
        "bpyc,bcx->bpyx", window, col_band, preferred_element_type=jnp.float32
    ).astype(jnp.bfloat16)
    padded = with_halo(filtered, (("raft", 2),), half_width)
    row_band = tap_band(row_taps, wide_index[None, :] - narrow[:, None])
    stacked = jnp.einsum("byr,bprx->pyx", row_band, padded, preferred_element_type=jnp.float32)
    summed, weight_total = (
        lax.psum_scatter(stacked, "visit", scatter_dimension=0, tiled=True),
        lax.psum_scatter(weight_sum, "visit", scatter_dimension=0, tiled=True),
    )
    coadd_image = summed / (1.0 + weight_total)[:, None, None]
    return coadd_image[None]


def filter_kernel(mix_ref, got_ref, col_ref, row_ref, out_ref, planes, strip, filtered, total):
    step = pl.program_id(0)
    count = GROUP * PATCH_DEV
    lines = got_ref.shape[1] // SIDE
    blocks = PATCH_DEV + 1

    def make_planes(pair, carry):
        start = pl.multiple_of(pair * 2 * SIDE, 2 * SIDE)
        both = jnp.dot(
            mix_ref[...], got_ref[:, pl.ds(start, 2 * SIDE)], preferred_element_type=jnp.float32
        )
        row = pl.multiple_of(pair * 2 * count, 8)
        planes[pl.ds(row, count), :] = both[:, :SIDE]
        planes[pl.ds(pl.multiple_of(row + count, 8), count), :] = both[:, SIDE:]
        return carry

    lax.fori_loop(0, lines // 2, make_planes, 0, unroll=4)

    @pl.when(step == 0)
    def _():
        strip[:, :SIDE] = jnp.zeros((lines, SIDE), jnp.bfloat16)
        strip[:, (PATCH_DEV + 1) * SIDE :] = jnp.zeros((lines, SIDE), jnp.bfloat16)

    def filter_columns(basis, carry):
        for place in range(PATCH_DEV):
            image = planes[pl.ds(basis * PATCH_DEV + place, lines, stride=count), :]
            strip[:, (place + 1) * SIDE : (place + 2) * SIDE] = image.astype(jnp.bfloat16)
        rows = pl.ds(pl.multiple_of(basis * lines, 16), lines)
        for block in range(blocks):
            wide = strip[:, block * SIDE : (block + 2) * SIDE]
            filtered[rows, block * SIDE : (block + 1) * SIDE] = jnp.dot(
                wide, col_ref[basis], preferred_element_type=jnp.float32
            ).astype(jnp.bfloat16)
        return carry

    lax.fori_loop(0, GROUP, filter_columns, 0)

    width = 5 * SIDE
    for chunk in range(blocks // 5):
        span = slice(chunk * width, (chunk + 1) * width)
        part = jnp.dot(row_ref[0], filtered[:, span], preferred_element_type=jnp.float32)
        total[:, span] = jnp.where(step == 0, part, total[:, span] + part)

    @pl.when(step == NB // GROUP - 1)
    def _():
        for place in range(PATCH_DEV):
            low = place * SIDE + SIDE // 2
            out_ref[place] = total[:, low : low + SIDE].astype(jnp.bfloat16)


def filter_tiles(mix, got, col_band, row_band):
    slots, pixels = got.shape
    lines = pixels // SIDE
    steps = NB // GROUP
    count = GROUP * PATCH_DEV
    width = (PATCH_DEV + 1) * SIDE
    return pl.pallas_call(
        filter_kernel,
        grid=(steps,),
        out_shape=jax.ShapeDtypeStruct((PATCH_DEV, OUT_ROWS, SIDE), jnp.bfloat16),
        in_specs=[
            pl.BlockSpec((count, slots), lambda s: (s, 0)),
            pl.BlockSpec((slots, pixels), lambda s: (0, 0)),
            pl.BlockSpec((GROUP, 2 * SIDE, SIDE), lambda s: (s, 0, 0)),
            pl.BlockSpec((1, OUT_ROWS, GROUP * lines), lambda s: (s, 0, 0)),
        ],
        out_specs=pl.BlockSpec((PATCH_DEV, OUT_ROWS, SIDE), lambda s: (0, 0, 0)),
        scratch_shapes=[
            pltpu.VMEM((lines * count, SIDE), jnp.float32),
            pltpu.VMEM((lines, (PATCH_DEV + 2) * SIDE), jnp.bfloat16),
            pltpu.VMEM((GROUP * lines, width), jnp.bfloat16),
            pltpu.VMEM((OUT_ROWS, width), jnp.float32),
        ],
        compiler_params=pltpu.CompilerParams(vmem_limit_bytes=56 * 1024 * 1024),
        cost_estimate=pl.CostEstimate(
            flops=30_000_000_000, bytes_accessed=10_000_000, transcendentals=0
        ),
    )(mix, got, col_band, row_band)


def plane_body(visits, depth, cores, tiles, weights, coef, owner, patch, row_taps, col_taps):
    tile_count = tiles.shape[0]
    owners = depth * cores
    capacity = 2 * tile_count // owners
    every = ("visit", "z", "core")
    owner_ids = owner[:, 0]
    plain_weight = weights.astype(jnp.bfloat16).astype(jnp.float32)
    keys = owner_ids * PATCH_DEV + patch
    key_hits = keys[:, None] == jnp.arange(owners * PATCH_DEV)[None, :]
    weight_sum = jnp.sum(jnp.where(key_hits, plain_weight[:, None], 0.0), axis=0)
    weight_total = lax.psum(weight_sum, every)
    strip_id = lax.axis_index("z") * cores + lax.axis_index("core")
    share = PATCH_DEV // visits
    own_weight = lax.dynamic_slice(
        weight_total, (strip_id * PATCH_DEV + lax.axis_index("visit") * share,), (share,)
    )

    owner_hits = (owner_ids[:, None] == jnp.arange(owners)[None, :]).astype(jnp.int32)
    slot_rank = jnp.sum(jnp.cumsum(owner_hits, axis=0) * owner_hits, axis=1) - 1
    slot_index = owner_ids * capacity + slot_rank
    placing = (jnp.arange(owners * capacity)[:, None] == slot_index[None, :]).astype(jnp.bfloat16)
    scaled = (weights[:, None] * coef).astype(jnp.bfloat16)
    patch_hits = (patch[:, None] == jnp.arange(PATCH_DEV)[None, :]).astype(jnp.bfloat16)
    blank = jnp.zeros((tile_count, SIDE - NB - PATCH_DEV), jnp.bfloat16)
    terms = jnp.concatenate([scaled, patch_hits, blank], axis=1)
    send_terms = jnp.dot(placing, terms, preferred_element_type=jnp.float32).astype(jnp.bfloat16)
    send_tiles = jnp.dot(placing, tiles, preferred_element_type=jnp.float32).astype(jnp.bfloat16)
    plane = ("visit", "core")
    got_terms = lax.all_to_all(send_terms, plane, split_axis=0, concat_axis=0, tiled=True)
    got_tiles = lax.all_to_all(send_tiles, plane, split_axis=0, concat_axis=0, tiled=True)
    by_basis = got_terms[:, :NB].T
    by_patch = got_terms[:, NB : NB + PATCH_DEV].T
    mix = (by_basis[:, None, :] * by_patch[None, :, :]).reshape(NB * PATCH_DEV, -1)

    wide_index = jnp.arange(2 * SIDE)
    narrow = jnp.arange(SIDE)
    col_band = tap_band(col_taps, wide_index[:, None] - narrow[None, :] - SIDE // 2 + HALF)
    out_index = jnp.arange(OUT_ROWS)
    row_band = tap_band(row_taps, narrow[None, :] - out_index[:, None] + TOP + HALF)
    row_band = row_band.reshape(NB // GROUP, GROUP, OUT_ROWS, SIDE).transpose(0, 2, 1, 3)
    row_band = row_band.reshape(NB // GROUP, OUT_ROWS, GROUP * SIDE)
    stacked = filter_tiles(mix, got_tiles, col_band, row_band)

    parts = lax.all_to_all(stacked, "z", split_axis=0, concat_axis=0, tiled=True)
    parts = parts.reshape(depth, share, OUT_ROWS, SIDE)
    summed = jnp.sum(parts.astype(jnp.float32), axis=0).astype(jnp.bfloat16)

    def to_owner(values, shift):
        pairs = []
        for v in range(visits):
            for q in range(depth):
                for c in range(cores):
                    target = v * cores + c + shift
                    if 0 <= target < owners:
                        pairs.append(((v * depth + q) * cores + c, q * owners + target))
        return lax.ppermute(values, every, pairs).astype(jnp.float32)

    center = to_owner(summed[:, TOP : TOP + SIDE], 0)
    lower = to_owner(summed[:, TOP - HALF : TOP], -1)
    upper = to_owner(summed[:, TOP + SIDE : TOP + SIDE + HALF], 1)
    rest = ((0, 0), (0, SIDE - HALF), (0, 0))
    numerator = center + jnp.pad(upper, rest)
    numerator = numerator + jnp.pad(lower, ((0, 0), (SIDE - HALF, 0), (0, 0)))
    return (numerator / (1.0 + own_weight)[:, None, None])[None]


def solution(mesh):
    visits, rafts = mesh.shape["visit"], mesh.shape["raft"]
    cores = 2
    if visits * cores == rafts and PATCH_DEV % visits == 0:
        depth = rafts // cores
        split = Mesh(mesh.devices.reshape(visits, depth, cores), ("visit", "z", "core"))
        every = ("visit", "z", "core")
        placed = (P(every, None), P(every), P(every, None), P(every, None), P(every), P(), P())
        return jax.shard_map(
            functools.partial(plane_body, visits, depth, cores),
            mesh=split,
            in_specs=placed,
            out_specs=P(("z", "core"), "visit", None, None),
            check_vma=False,
        )
    placed = (
        P(("visit", "raft"), None),
        P(("visit", "raft")),
        P(("visit", "raft"), None),
        P(("visit", "raft"), None),
        P(("visit", "raft")),
        P(),
        P(),
    )
    return jax.shard_map(
        body, mesh=mesh, in_specs=placed, out_specs=P("raft", "visit", None, None), check_vma=False
    )
```

```python
import functools

import jax
import jax.numpy as jnp
from jax import lax
from jax.experimental import pallas as pl
from jax.experimental.pallas import tpu as pltpu
from jax.sharding import Mesh, PartitionSpec as P

SIDE = 128
KERNEL = 41
NB = 27
PATCH_DEV = 24
GROUP = 9
HALF = (KERNEL - 1) // 2
TOP = 24
OUT_ROWS = 176
FIRST = 80


def with_halo(shard, sides, width):
    for axis, dim in sides:
        size, length = (lax.axis_size(axis), shard.shape[dim])
        up = [(i, (i + 1) % size) for i in range(size - 1)]
        down = [(j, i) for i, j in up]
        last = lax.slice_in_dim(shard, length - width, length, axis=dim)
        leading = lax.slice_in_dim(shard, 0, width, axis=dim)
        before = lax.ppermute(last, axis, up)
        after = lax.ppermute(leading, axis, down)
        shard = jnp.concatenate([before, shard, after], axis=dim)
    return shard


def tap_band(tap_values, offsets):
    selector = (offsets[:, :, None] == jnp.arange(tap_values.shape[1])[None, None, :]).astype(
        jnp.float32
    )
    return jnp.einsum("qrj,bj->bqr", selector, tap_values.astype(jnp.float32)).astype(jnp.bfloat16)


def body(tiles, weights, coef, owner, patch, row_taps, col_taps):
    tile_count = tiles.shape[0]
    peer_count = lax.axis_size("raft")
    capacity = max(2, 2 * tile_count // peer_count)
    half_width = (KERNEL - 1) // 2
    owner_ids = owner[:, 0]
    owner_hits = (owner_ids[:, None] == jnp.arange(peer_count)[None, :]).astype(jnp.int32)
    slot_rank = jnp.sum(jnp.cumsum(owner_hits, axis=0) * owner_hits, axis=1) - 1
    slot_index = owner_ids * capacity + slot_rank
    placing = (jnp.arange(peer_count * capacity)[:, None] == slot_index[None, :]).astype(
        jnp.bfloat16
    )
    scaled = (weights[:, None] * coef).astype(jnp.bfloat16)
    plain_weight = weights.astype(jnp.bfloat16)[:, None]
    tile_terms = jnp.concatenate([scaled, plain_weight], axis=1)
    patch_hits = (patch[:, None] == jnp.arange(PATCH_DEV)[None, :]).astype(jnp.bfloat16)
    mixing = (tile_terms[:, :, None] * patch_hits[:, None, :]).reshape(
        tile_count, (NB + 1) * PATCH_DEV
    )
    send_tiles = jnp.dot(placing, tiles, preferred_element_type=jnp.float32).astype(jnp.bfloat16)
    send_mixing = jnp.dot(placing, mixing, preferred_element_type=jnp.float32).astype(jnp.bfloat16)
    got_tiles, got_mixing = (
        lax.all_to_all(send_tiles, "raft", split_axis=0, concat_axis=0, tiled=True),
        lax.all_to_all(send_mixing, "raft", split_axis=0, concat_axis=0, tiled=True),
    )
    planes = lax.dot_general(
        got_mixing[:, : NB * PATCH_DEV],
        got_tiles,
        (((0,), (0,)), ((), ())),
        preferred_element_type=jnp.float32,
    )
    planes = planes.astype(jnp.bfloat16).reshape(NB, PATCH_DEV, SIDE, SIDE)
    weight_sum = jnp.sum(got_mixing[:, NB * PATCH_DEV :].astype(jnp.float32), axis=0)
    blank_rim = jnp.zeros((NB, 1, SIDE, half_width), jnp.bfloat16)
    left_rim = jnp.concatenate([blank_rim, planes[:, :-1, :, SIDE - half_width :]], axis=1)
    right_rim = jnp.concatenate([planes[:, 1:, :, :half_width], blank_rim], axis=1)
    window = jnp.concatenate([left_rim, planes, right_rim], axis=3)
    wide_index = jnp.arange(SIDE + 2 * half_width)
    narrow = jnp.arange(SIDE)
    col_band = tap_band(col_taps, wide_index[:, None] - narrow[None, :])
    filtered = jnp.einsum(
        "bpyc,bcx->bpyx", window, col_band, preferred_element_type=jnp.float32
    ).astype(jnp.bfloat16)
    padded = with_halo(filtered, (("raft", 2),), half_width)
    row_band = tap_band(row_taps, wide_index[None, :] - narrow[:, None])
    stacked = jnp.einsum("byr,bprx->pyx", row_band, padded, preferred_element_type=jnp.float32)
    summed, weight_total = (
        lax.psum_scatter(stacked, "visit", scatter_dimension=0, tiled=True),
        lax.psum_scatter(weight_sum, "visit", scatter_dimension=0, tiled=True),
    )
    coadd_image = summed / (1.0 + weight_total)[:, None, None]
    return coadd_image[None]


def filter_kernel(final, lines, mix_ref, got_ref, col_ref, row_ref, *rest):
    if final:
        before_ref, weight_ref, out_ref, planes, strip, filtered, total = rest
    else:
        total, planes, strip, filtered = rest
    step = pl.program_id(0)
    count = GROUP * PATCH_DEV
    blocks = PATCH_DEV + 1

    def make_planes(pair, carry):
        start = pl.multiple_of(pair * 2 * SIDE, 2 * SIDE)
        both = jnp.dot(
            mix_ref[...], got_ref[:, pl.ds(start, 2 * SIDE)], preferred_element_type=jnp.float32
        )
        row = pl.multiple_of(pair * 2 * count, 8)
        planes[pl.ds(row, count), :] = both[:, :SIDE]
        planes[pl.ds(pl.multiple_of(row + count, 8), count), :] = both[:, SIDE:]
        return carry

    lax.fori_loop(0, lines // 2, make_planes, 0, unroll=4)

    @pl.when(step == 0)
    def _():
        strip[:lines, :SIDE] = jnp.zeros((lines, SIDE), jnp.bfloat16)
        strip[PATCH_DEV * lines :, SIDE:] = jnp.zeros((lines, SIDE), jnp.bfloat16)

    def filter_columns(basis, carry):
        for place in range(PATCH_DEV):
            image = planes[pl.ds(basis * PATCH_DEV + place, lines, stride=count), :]
            image = image.astype(jnp.bfloat16)
            strip[place * lines : (place + 1) * lines, SIDE:] = image
            strip[(place + 1) * lines : (place + 2) * lines, :SIDE] = image
        rows = pl.ds(pl.multiple_of(basis * lines, 16), lines)
        for first in range(0, blocks, 5):
            wide = jnp.dot(
                strip[first * lines : (first + 5) * lines, :],
                col_ref[basis],
                preferred_element_type=jnp.float32,
            ).astype(jnp.bfloat16)
            for block in range(5):
                low = (first + block) * SIDE
                filtered[rows, low : low + SIDE] = wide[block * lines : (block + 1) * lines]
        return carry

    lax.fori_loop(0, GROUP, filter_columns, 0)

    width = 5 * SIDE
    for chunk in range(blocks // 5):
        span = slice(chunk * width, (chunk + 1) * width)
        part = jnp.dot(row_ref[0], filtered[:, span], preferred_element_type=jnp.float32)
        start = before_ref[:, span] if final else 0.0
        total[:, span] = part + jnp.where(step == 0, start, total[:, span])

    if final:

        @pl.when(step == NB // GROUP - 1)
        def _():
            for place in range(PATCH_DEV):
                low = place * SIDE + SIDE // 2
                image = total[:, low : low + SIDE]
                out_ref[place, :16] = (image[:16] + weight_ref[place]).astype(jnp.bfloat16)
                out_ref[place, 16:] = image[16:].astype(jnp.bfloat16)


def filter_tiles(lines, mix, got, col_band, row_band, before=None, weight=None):
    slots, pixels = got.shape
    steps = NB // GROUP
    count = GROUP * PATCH_DEV
    blocks = PATCH_DEV + 1
    final = before is not None
    args = [mix, got, col_band, row_band]
    in_specs = [
        pl.BlockSpec((count, slots), lambda s: (s, 0)),
        pl.BlockSpec((slots, pixels), lambda s: (0, 0)),
        pl.BlockSpec((GROUP, 2 * SIDE, SIDE), lambda s: (s, 0, 0)),
        pl.BlockSpec((1, OUT_ROWS, GROUP * lines), lambda s: (s, 0, 0)),
    ]
    whole = pl.BlockSpec((OUT_ROWS, blocks * SIDE), lambda s: (0, 0))
    scratch = [
        pltpu.VMEM((lines * count, SIDE), jnp.float32),
        pltpu.VMEM((blocks * lines, 2 * SIDE), jnp.bfloat16),
        pltpu.VMEM((GROUP * lines, blocks * SIDE), jnp.bfloat16),
    ]
    out_shape = jax.ShapeDtypeStruct((OUT_ROWS, blocks * SIDE), jnp.float32)
    out_specs = whole
    if final:
        args += [before, weight]
        in_specs += [whole, pl.BlockSpec((PATCH_DEV, 16, SIDE), lambda s: (0, 0, 0))]
        scratch += [pltpu.VMEM((OUT_ROWS, blocks * SIDE), jnp.float32)]
        out_shape = jax.ShapeDtypeStruct((PATCH_DEV, OUT_ROWS, SIDE), jnp.bfloat16)
        out_specs = pl.BlockSpec((PATCH_DEV, OUT_ROWS, SIDE), lambda s: (0, 0, 0))
    return pl.pallas_call(
        functools.partial(filter_kernel, final, lines),
        grid=(steps,),
        out_shape=out_shape,
        in_specs=in_specs,
        out_specs=out_specs,
        scratch_shapes=scratch,
        compiler_params=pltpu.CompilerParams(vmem_limit_bytes=56 * 1024 * 1024),
        cost_estimate=pl.CostEstimate(
            flops=200_000_000 * lines, bytes_accessed=100_000 * lines, transcendentals=0
        ),
    )(*args)


def plane_body(visits, depth, cores, tiles, weights, coef, owner, patch, row_taps, col_taps):
    tile_count = tiles.shape[0]
    owners = depth * cores
    capacity = 2 * tile_count // owners
    every = ("visit", "z", "core")
    owner_ids = owner[:, 0]
    share = PATCH_DEV // visits
    plain_weight = weights.astype(jnp.bfloat16)[:, None]
    owner_hits = (owner_ids[:, None] == jnp.arange(owners)[None, :]).astype(jnp.int32)
    slot_rank = jnp.sum(jnp.cumsum(owner_hits, axis=0) * owner_hits, axis=1) - 1
    slot_index = owner_ids * capacity + slot_rank
    placing = (jnp.arange(owners * capacity)[:, None] == slot_index[None, :]).astype(jnp.bfloat16)
    scaled = (weights[:, None] * coef).astype(jnp.bfloat16)
    patch_hits = (patch[:, None] == jnp.arange(PATCH_DEV)[None, :]).astype(jnp.bfloat16)
    blank = jnp.zeros((tile_count, SIDE - NB - PATCH_DEV - 1), jnp.bfloat16)
    terms = jnp.concatenate([scaled, patch_hits, plain_weight, blank], axis=1)

    def place(values):
        return jnp.dot(placing, values, preferred_element_type=jnp.float32).astype(jnp.bfloat16)

    def exchange(values):
        return lax.all_to_all(
            values, ("visit", "core"), split_axis=0, concat_axis=0, tiled=True
        )

    cut = FIRST * SIDE
    got_first = exchange(place(jnp.concatenate([tiles[:, :cut], terms], axis=1)))
    got_first, held = lax.optimization_barrier((got_first, place(tiles[:, cut:])))
    got_second = exchange(held)
    got_terms = got_first[:, cut:]
    by_basis = got_terms[:, :NB].T
    hits = got_terms[:, NB : NB + PATCH_DEV]
    mix = (by_basis[:, None, :] * hits.T[None, :, :]).reshape(NB * PATCH_DEV, -1)
    got_weight = got_terms[:, NB + PATCH_DEV :][:, :1].astype(jnp.float32)
    weight_sum = jnp.sum(got_weight * hits.astype(jnp.float32), axis=0)
    high = lax.reduce_precision(weight_sum, 8, 7)
    halves = jnp.stack([high, weight_sum - high], axis=1)
    weight_rows = jnp.pad(halves, ((0, 0), (0, 14)))[:, :, None]
    weight_rows = jnp.broadcast_to(weight_rows, (PATCH_DEV, 16, SIDE))

    wide_index = jnp.arange(2 * SIDE)
    narrow = jnp.arange(SIDE)
    col_band = tap_band(col_taps, wide_index[:, None] - narrow[None, :] - SIDE // 2 + HALF)
    out_index = jnp.arange(OUT_ROWS)
    row_band = tap_band(row_taps, narrow[None, :] - out_index[:, None] + TOP + HALF)
    row_band = row_band.reshape(NB // GROUP, GROUP, OUT_ROWS, SIDE).transpose(0, 2, 1, 3)
    row_first = row_band[..., :FIRST].reshape(NB // GROUP, OUT_ROWS, -1)
    row_second = row_band[..., FIRST:].reshape(NB // GROUP, OUT_ROWS, -1)
    partial = filter_tiles(FIRST, mix, got_first, col_band, row_first)
    stacked = filter_tiles(
        SIDE - FIRST, mix, got_second, col_band, row_second, partial, weight_rows
    )

    parts = lax.all_to_all(stacked, "z", split_axis=0, concat_axis=0, tiled=True)
    parts = parts.reshape(depth, share, OUT_ROWS, SIDE).astype(jnp.float32)
    summed = jnp.sum(parts, axis=0).astype(jnp.bfloat16)
    plane_weight = jnp.sum(parts[:, :, :2], axis=(0, 2))

    def to_owner(values, shift):
        pairs = []
        for v in range(visits):
            for q in range(depth):
                for c in range(cores):
                    target = v * cores + c + shift
                    if 0 <= target < owners:
                        pairs.append(((v * depth + q) * cores + c, q * owners + target))
        return lax.ppermute(values, every, pairs).astype(jnp.float32)

    center = to_owner(summed[:, TOP : TOP + SIDE], 0)
    lower = to_owner(summed[:, TOP - HALF : TOP], -1)
    upper = to_owner(summed[:, TOP + SIDE : TOP + SIDE + HALF], 1)
    own_weight = to_owner(plane_weight, 0)
    rest = ((0, 0), (0, SIDE - HALF), (0, 0))
    numerator = center + jnp.pad(upper, rest)
    numerator = numerator + jnp.pad(lower, ((0, 0), (SIDE - HALF, 0), (0, 0)))
    return (numerator / (1.0 + own_weight)[:, None, :])[None]


def solution(mesh):
    visits, rafts = mesh.shape["visit"], mesh.shape["raft"]
    cores = 2
    if visits * cores == rafts and PATCH_DEV % visits == 0:
        depth = rafts // cores
        split = Mesh(mesh.devices.reshape(visits, depth, cores), ("visit", "z", "core"))
        every = ("visit", "z", "core")
        placed = (P(every, None), P(every), P(every, None), P(every, None), P(every), P(), P())
        return jax.shard_map(
            functools.partial(plane_body, visits, depth, cores),
            mesh=split,
            in_specs=placed,
            out_specs=P(("z", "core"), "visit", None, None),
            check_vma=False,
        )
    placed = (
        P(("visit", "raft"), None),
        P(("visit", "raft")),
        P(("visit", "raft"), None),
        P(("visit", "raft"), None),
        P(("visit", "raft")),
        P(),
        P(),
    )
    return jax.shard_map(
        body, mesh=mesh, in_specs=placed, out_specs=P("raft", "visit", None, None), check_vma=False
    )
```

```python
import functools

import jax
import jax.numpy as jnp
from jax import lax
from jax.experimental import pallas as pl
from jax.experimental.pallas import tpu as pltpu
from jax.sharding import Mesh, PartitionSpec as P

SIDE = 128
KERNEL = 41
NB = 27
PATCH_DEV = 24
GROUP = 9
HALF = (KERNEL - 1) // 2
TOP = 24
OUT_ROWS = 176
FIRST = 80


def with_halo(shard, sides, width):
    for axis, dim in sides:
        size, length = (lax.axis_size(axis), shard.shape[dim])
        up = [(i, (i + 1) % size) for i in range(size - 1)]
        down = [(j, i) for i, j in up]
        last = lax.slice_in_dim(shard, length - width, length, axis=dim)
        leading = lax.slice_in_dim(shard, 0, width, axis=dim)
        before = lax.ppermute(last, axis, up)
        after = lax.ppermute(leading, axis, down)
        shard = jnp.concatenate([before, shard, after], axis=dim)
    return shard


def tap_band(tap_values, offsets):
    selector = (offsets[:, :, None] == jnp.arange(tap_values.shape[1])[None, None, :]).astype(
        jnp.float32
    )
    return jnp.einsum("qrj,bj->bqr", selector, tap_values.astype(jnp.float32)).astype(jnp.bfloat16)


def body(tiles, weights, coef, owner, patch, row_taps, col_taps):
    tile_count = tiles.shape[0]
    peer_count = lax.axis_size("raft")
    capacity = max(2, 2 * tile_count // peer_count)
    half_width = (KERNEL - 1) // 2
    owner_ids = owner[:, 0]
    owner_hits = (owner_ids[:, None] == jnp.arange(peer_count)[None, :]).astype(jnp.int32)
    slot_rank = jnp.sum(jnp.cumsum(owner_hits, axis=0) * owner_hits, axis=1) - 1
    slot_index = owner_ids * capacity + slot_rank
    placing = (jnp.arange(peer_count * capacity)[:, None] == slot_index[None, :]).astype(
        jnp.bfloat16
    )
    scaled = (weights[:, None] * coef).astype(jnp.bfloat16)
    plain_weight = weights.astype(jnp.bfloat16)[:, None]
    tile_terms = jnp.concatenate([scaled, plain_weight], axis=1)
    patch_hits = (patch[:, None] == jnp.arange(PATCH_DEV)[None, :]).astype(jnp.bfloat16)
    mixing = (tile_terms[:, :, None] * patch_hits[:, None, :]).reshape(
        tile_count, (NB + 1) * PATCH_DEV
    )
    send_tiles = jnp.dot(placing, tiles, preferred_element_type=jnp.float32).astype(jnp.bfloat16)
    send_mixing = jnp.dot(placing, mixing, preferred_element_type=jnp.float32).astype(jnp.bfloat16)
    got_tiles, got_mixing = (
        lax.all_to_all(send_tiles, "raft", split_axis=0, concat_axis=0, tiled=True),
        lax.all_to_all(send_mixing, "raft", split_axis=0, concat_axis=0, tiled=True),
    )
    planes = lax.dot_general(
        got_mixing[:, : NB * PATCH_DEV],
        got_tiles,
        (((0,), (0,)), ((), ())),
        preferred_element_type=jnp.float32,
    )
    planes = planes.astype(jnp.bfloat16).reshape(NB, PATCH_DEV, SIDE, SIDE)
    weight_sum = jnp.sum(got_mixing[:, NB * PATCH_DEV :].astype(jnp.float32), axis=0)
    blank_rim = jnp.zeros((NB, 1, SIDE, half_width), jnp.bfloat16)
    left_rim = jnp.concatenate([blank_rim, planes[:, :-1, :, SIDE - half_width :]], axis=1)
    right_rim = jnp.concatenate([planes[:, 1:, :, :half_width], blank_rim], axis=1)
    window = jnp.concatenate([left_rim, planes, right_rim], axis=3)
    wide_index = jnp.arange(SIDE + 2 * half_width)
    narrow = jnp.arange(SIDE)
    col_band = tap_band(col_taps, wide_index[:, None] - narrow[None, :])
    filtered = jnp.einsum(
        "bpyc,bcx->bpyx", window, col_band, preferred_element_type=jnp.float32
    ).astype(jnp.bfloat16)
    padded = with_halo(filtered, (("raft", 2),), half_width)
    row_band = tap_band(row_taps, wide_index[None, :] - narrow[:, None])
    stacked = jnp.einsum("byr,bprx->pyx", row_band, padded, preferred_element_type=jnp.float32)
    summed, weight_total = (
        lax.psum_scatter(stacked, "visit", scatter_dimension=0, tiled=True),
        lax.psum_scatter(weight_sum, "visit", scatter_dimension=0, tiled=True),
    )
    coadd_image = summed / (1.0 + weight_total)[:, None, None]
    return coadd_image[None]


def filter_kernel(final, lines, mix_ref, got_ref, col_ref, row_ref, *rest):
    if final:
        before_ref, out_ref, planes, strip, filtered, total = rest
    else:
        weight_ref, out_ref, after_ref, planes, strip, filtered, total = rest
    step = pl.program_id(0)
    count = GROUP * PATCH_DEV
    blocks = PATCH_DEV + 1

    def make_planes(pair, carry):
        start = pl.multiple_of(pair * 2 * SIDE, 2 * SIDE)
        both = jnp.dot(
            mix_ref[...], got_ref[:, pl.ds(start, 2 * SIDE)], preferred_element_type=jnp.float32
        )
        row = pl.multiple_of(pair * 2 * count, 8)
        planes[pl.ds(row, count), :] = both[:, :SIDE]
        planes[pl.ds(pl.multiple_of(row + count, 8), count), :] = both[:, SIDE:]
        return carry

    lax.fori_loop(0, lines // 2, make_planes, 0, unroll=4)

    @pl.when(step == 0)
    def _():
        strip[:lines, :SIDE] = jnp.zeros((lines, SIDE), jnp.bfloat16)
        strip[PATCH_DEV * lines :, SIDE:] = jnp.zeros((lines, SIDE), jnp.bfloat16)

    def filter_columns(basis, carry):
        for place in range(PATCH_DEV):
            image = planes[pl.ds(basis * PATCH_DEV + place, lines, stride=count), :]
            image = image.astype(jnp.bfloat16)
            strip[place * lines : (place + 1) * lines, SIDE:] = image
            strip[(place + 1) * lines : (place + 2) * lines, :SIDE] = image
        rows = pl.ds(pl.multiple_of(basis * lines, 16), lines)
        wide = jnp.dot(strip[...], col_ref[basis], preferred_element_type=jnp.float32)
        wide = wide.astype(jnp.bfloat16)
        for block in range(blocks):
            low = block * SIDE
            filtered[rows, low : low + SIDE] = wide[block * lines : (block + 1) * lines]
        return carry

    lax.fori_loop(0, GROUP, filter_columns, 0)

    width = 5 * SIDE
    for chunk in range(blocks // 5):
        span = slice(chunk * width, (chunk + 1) * width)
        part = jnp.dot(row_ref[0], filtered[:, span], preferred_element_type=jnp.float32)
        start = before_ref[:, span] if final else 0.0
        total[:, span] = part + jnp.where(step == 0, start, total[:, span])

    @pl.when(step == NB // GROUP - 1)
    def _():
        ready = out_ref.shape[1]
        for place in range(PATCH_DEV):
            low = place * SIDE + SIDE // 2
            image = total[:ready, low : low + SIDE]
            if final:
                out_ref[place] = image.astype(jnp.bfloat16)
            else:
                out_ref[place, :16] = (image[:16] + weight_ref[place]).astype(jnp.bfloat16)
                out_ref[place, 16:] = image[16:].astype(jnp.bfloat16)
        if not final:
            after_ref[...] = total[ready:, :]


def place_kernel(placing_ref, tiles_ref, terms_ref, out_ref):
    out_ref[...] = jnp.dot(
        placing_ref[...], tiles_ref[...], preferred_element_type=jnp.float32
    ).astype(jnp.bfloat16)

    @pl.when(pl.program_id(0) == pl.num_programs(0) - 1)
    def _():
        last = out_ref.shape[1] - SIDE
        out_ref[:, last:] = jnp.dot(
            placing_ref[...], terms_ref[...], preferred_element_type=jnp.float32
        ).astype(jnp.bfloat16)


def place_first(placing, tiles, terms):
    slots, tile_count = placing.shape
    steps = 9
    width = (FIRST + 1) * SIDE // steps
    return pl.pallas_call(
        place_kernel,
        grid=(steps,),
        out_shape=jax.ShapeDtypeStruct((slots, steps * width), jnp.bfloat16),
        in_specs=[
            pl.BlockSpec((slots, tile_count), lambda s: (0, 0)),
            pl.BlockSpec((tile_count, width), lambda s: (0, s)),
            pl.BlockSpec((tile_count, SIDE), lambda s: (0, 0)),
        ],
        out_specs=pl.BlockSpec((slots, width), lambda s: (0, s)),
        compiler_params=pltpu.CompilerParams(vmem_limit_bytes=16 * 1024 * 1024),
        cost_estimate=pl.CostEstimate(
            flops=2 * slots * tile_count * steps * width,
            bytes_accessed=2 * (slots + tile_count) * steps * width,
            transcendentals=0,
        ),
    )(placing, tiles, terms)


def filter_tiles(lines, mix, got, col_band, row_band, before=None, weight=None):
    slots, pixels = got.shape
    steps = NB // GROUP
    count = GROUP * PATCH_DEV
    blocks = PATCH_DEV + 1
    final = before is not None
    rows = row_band.shape[1]
    args = [mix, got, col_band, row_band]
    in_specs = [
        pl.BlockSpec((count, slots), lambda s: (s, 0)),
        pl.BlockSpec((slots, pixels), lambda s: (0, 0)),
        pl.BlockSpec((GROUP, 2 * SIDE, SIDE), lambda s: (s, 0, 0)),
        pl.BlockSpec((1, rows, GROUP * lines), lambda s: (s, 0, 0)),
    ]
    later = pl.BlockSpec((OUT_ROWS - FIRST, blocks * SIDE), lambda s: (0, 0))
    scratch = [
        pltpu.VMEM((lines * count, SIDE), jnp.float32),
        pltpu.VMEM((blocks * lines, 2 * SIDE), jnp.bfloat16),
        pltpu.VMEM((GROUP * lines, blocks * SIDE), jnp.bfloat16),
        pltpu.VMEM((rows, blocks * SIDE), jnp.float32),
    ]
    ready = rows if final else FIRST
    out_shape = [jax.ShapeDtypeStruct((PATCH_DEV, ready, SIDE), jnp.bfloat16)]
    out_specs = [pl.BlockSpec((PATCH_DEV, ready, SIDE), lambda s: (0, 0, 0))]
    if final:
        args += [before]
        in_specs += [later]
    else:
        args += [weight]
        in_specs += [pl.BlockSpec((PATCH_DEV, 16, SIDE), lambda s: (0, 0, 0))]
        out_shape += [jax.ShapeDtypeStruct((OUT_ROWS - FIRST, blocks * SIDE), jnp.float32)]
        out_specs += [later]
    return pl.pallas_call(
        functools.partial(filter_kernel, final, lines),
        grid=(steps,),
        out_shape=out_shape,
        in_specs=in_specs,
        out_specs=out_specs,
        scratch_shapes=scratch,
        compiler_params=pltpu.CompilerParams(vmem_limit_bytes=56 * 1024 * 1024),
        cost_estimate=pl.CostEstimate(
            flops=200_000_000 * lines, bytes_accessed=100_000 * lines, transcendentals=0
        ),
    )(*args)


def plane_body(visits, depth, cores, tiles, weights, coef, owner, patch, row_taps, col_taps):
    tile_count = tiles.shape[0]
    owners = depth * cores
    capacity = 2 * tile_count // owners
    every = ("visit", "z", "core")
    owner_ids = owner[:, 0]
    share = PATCH_DEV // visits
    plain_weight = weights.astype(jnp.bfloat16)[:, None]
    owner_hits = (owner_ids[:, None] == jnp.arange(owners)[None, :]).astype(jnp.int32)
    slot_rank = jnp.sum(jnp.cumsum(owner_hits, axis=0) * owner_hits, axis=1) - 1
    slot_index = owner_ids * capacity + slot_rank
    placing = (jnp.arange(owners * capacity)[:, None] == slot_index[None, :]).astype(jnp.bfloat16)
    scaled = (weights[:, None] * coef).astype(jnp.bfloat16)
    patch_hits = (patch[:, None] == jnp.arange(PATCH_DEV)[None, :]).astype(jnp.bfloat16)
    blank = jnp.zeros((tile_count, SIDE - NB - PATCH_DEV - 1), jnp.bfloat16)
    terms = jnp.concatenate([scaled, patch_hits, plain_weight, blank], axis=1)

    def place(values):
        return jnp.dot(placing, values, preferred_element_type=jnp.float32).astype(jnp.bfloat16)

    def exchange(values):
        return lax.all_to_all(
            values, ("visit", "core"), split_axis=0, concat_axis=0, tiled=True
        )

    cut = FIRST * SIDE
    got_first = exchange(place_first(placing, tiles, terms))
    got_first, held = lax.optimization_barrier((got_first, place(tiles[:, cut:])))
    got_second = exchange(held)
    got_terms = got_first[:, cut:]
    by_basis = got_terms[:, :NB].T
    hits = got_terms[:, NB : NB + PATCH_DEV]
    mix = (by_basis[:, None, :] * hits.T[None, :, :]).reshape(NB * PATCH_DEV, -1)
    got_weight = got_terms[:, NB + PATCH_DEV :][:, :1].astype(jnp.float32)
    weight_sum = jnp.sum(got_weight * hits.astype(jnp.float32), axis=0)
    high = lax.reduce_precision(weight_sum, 8, 7)
    halves = jnp.stack([high, weight_sum - high], axis=1)
    weight_rows = jnp.pad(halves, ((0, 0), (0, 14)))[:, :, None]
    weight_rows = jnp.broadcast_to(weight_rows, (PATCH_DEV, 16, SIDE))

    wide_index = jnp.arange(2 * SIDE)
    narrow = jnp.arange(SIDE)
    col_band = tap_band(col_taps, wide_index[:, None] - narrow[None, :] - SIDE // 2 + HALF)
    out_index = jnp.arange(OUT_ROWS)
    row_band = tap_band(row_taps, narrow[None, :] - out_index[:, None] + TOP + HALF)
    row_band = row_band.reshape(NB // GROUP, GROUP, OUT_ROWS, SIDE).transpose(0, 2, 1, 3)
    row_first = row_band[..., :FIRST].reshape(NB // GROUP, OUT_ROWS, -1)
    row_second = row_band[:, FIRST:, :, FIRST:].reshape(NB // GROUP, OUT_ROWS - FIRST, -1)
    early, partial = filter_tiles(
        FIRST, mix, got_first, col_band, row_first, weight=weight_rows
    )
    (late,) = filter_tiles(SIDE - FIRST, mix, got_second, col_band, row_second, before=partial)

    def to_shares(values):
        parts = lax.all_to_all(values, "z", split_axis=0, concat_axis=0, tiled=True)
        return parts.reshape(depth, share, -1, SIDE).astype(jnp.float32)

    parts = to_shares(early)
    plane_weight = jnp.sum(parts[:, :, :2], axis=(0, 2))
    summed = jnp.sum(parts, axis=0).astype(jnp.bfloat16)
    summed_late = jnp.sum(to_shares(late), axis=0).astype(jnp.bfloat16)

    def to_owner(values, shift):
        pairs = []
        for v in range(visits):
            for q in range(depth):
                for c in range(cores):
                    target = v * cores + c + shift
                    if 0 <= target < owners:
                        pairs.append(((v * depth + q) * cores + c, q * owners + target))
        return lax.ppermute(values, every, pairs).astype(jnp.float32)

    head = to_owner(summed[:, TOP:], 0)
    tail = to_owner(summed_late[:, : TOP + SIDE - FIRST], 0)
    center = jnp.concatenate([head, tail], axis=1)
    lower = to_owner(summed[:, TOP - HALF : TOP], -1)
    low = TOP + SIDE - FIRST
    upper = to_owner(summed_late[:, low : low + HALF], 1)
    own_weight = to_owner(plane_weight, 0)
    rest = ((0, 0), (0, SIDE - HALF), (0, 0))
    numerator = center + jnp.pad(upper, rest)
    numerator = numerator + jnp.pad(lower, ((0, 0), (SIDE - HALF, 0), (0, 0)))
    return (numerator / (1.0 + own_weight)[:, None, :])[None]


def solution(mesh):
    visits, rafts = mesh.shape["visit"], mesh.shape["raft"]
    cores = 2
    if visits * cores == rafts and PATCH_DEV % visits == 0:
        depth = rafts // cores
        split = Mesh(mesh.devices.reshape(visits, depth, cores), ("visit", "z", "core"))
        every = ("visit", "z", "core")
        placed = (P(every, None), P(every), P(every, None), P(every, None), P(every), P(), P())
        return jax.shard_map(
            functools.partial(plane_body, visits, depth, cores),
            mesh=split,
            in_specs=placed,
            out_specs=P(("z", "core"), "visit", None, None),
            check_vma=False,
        )
    placed = (
        P(("visit", "raft"), None),
        P(("visit", "raft")),
        P(("visit", "raft"), None),
        P(("visit", "raft"), None),
        P(("visit", "raft")),
        P(),
        P(),
    )
    return jax.shard_map(
        body, mesh=mesh, in_specs=placed, out_specs=P("raft", "visit", None, None), check_vma=False
    )
```

```python
import functools

import jax
import jax.numpy as jnp
from jax import lax
from jax.experimental import pallas as pl
from jax.experimental.pallas import tpu as pltpu
from jax.sharding import Mesh, PartitionSpec as P

SIDE = 128
KERNEL = 41
NB = 27
PATCH_DEV = 24
GROUP = 9
HALF = (KERNEL - 1) // 2
TOP = 24
OUT_ROWS = 176
FIRST = 80


def with_halo(shard, sides, width):
    for axis, dim in sides:
        size, length = (lax.axis_size(axis), shard.shape[dim])
        up = [(i, (i + 1) % size) for i in range(size - 1)]
        down = [(j, i) for i, j in up]
        last = lax.slice_in_dim(shard, length - width, length, axis=dim)
        leading = lax.slice_in_dim(shard, 0, width, axis=dim)
        before = lax.ppermute(last, axis, up)
        after = lax.ppermute(leading, axis, down)
        shard = jnp.concatenate([before, shard, after], axis=dim)
    return shard


def tap_band(tap_values, offsets):
    selector = (offsets[:, :, None] == jnp.arange(tap_values.shape[1])[None, None, :]).astype(
        jnp.float32
    )
    return jnp.einsum("qrj,bj->bqr", selector, tap_values.astype(jnp.float32)).astype(jnp.bfloat16)


def body(tiles, weights, coef, owner, patch, row_taps, col_taps):
    tile_count = tiles.shape[0]
    peer_count = lax.axis_size("raft")
    capacity = max(2, 2 * tile_count // peer_count)
    half_width = (KERNEL - 1) // 2
    owner_ids = owner[:, 0]
    owner_hits = (owner_ids[:, None] == jnp.arange(peer_count)[None, :]).astype(jnp.int32)
    slot_rank = jnp.sum(jnp.cumsum(owner_hits, axis=0) * owner_hits, axis=1) - 1
    slot_index = owner_ids * capacity + slot_rank
    placing = (jnp.arange(peer_count * capacity)[:, None] == slot_index[None, :]).astype(
        jnp.bfloat16
    )
    scaled = (weights[:, None] * coef).astype(jnp.bfloat16)
    plain_weight = weights.astype(jnp.bfloat16)[:, None]
    tile_terms = jnp.concatenate([scaled, plain_weight], axis=1)
    patch_hits = (patch[:, None] == jnp.arange(PATCH_DEV)[None, :]).astype(jnp.bfloat16)
    mixing = (tile_terms[:, :, None] * patch_hits[:, None, :]).reshape(
        tile_count, (NB + 1) * PATCH_DEV
    )
    send_tiles = jnp.dot(placing, tiles, preferred_element_type=jnp.float32).astype(jnp.bfloat16)
    send_mixing = jnp.dot(placing, mixing, preferred_element_type=jnp.float32).astype(jnp.bfloat16)
    got_tiles, got_mixing = (
        lax.all_to_all(send_tiles, "raft", split_axis=0, concat_axis=0, tiled=True),
        lax.all_to_all(send_mixing, "raft", split_axis=0, concat_axis=0, tiled=True),
    )
    planes = lax.dot_general(
        got_mixing[:, : NB * PATCH_DEV],
        got_tiles,
        (((0,), (0,)), ((), ())),
        preferred_element_type=jnp.float32,
    )
    planes = planes.astype(jnp.bfloat16).reshape(NB, PATCH_DEV, SIDE, SIDE)
    weight_sum = jnp.sum(got_mixing[:, NB * PATCH_DEV :].astype(jnp.float32), axis=0)
    blank_rim = jnp.zeros((NB, 1, SIDE, half_width), jnp.bfloat16)
    left_rim = jnp.concatenate([blank_rim, planes[:, :-1, :, SIDE - half_width :]], axis=1)
    right_rim = jnp.concatenate([planes[:, 1:, :, :half_width], blank_rim], axis=1)
    window = jnp.concatenate([left_rim, planes, right_rim], axis=3)
    wide_index = jnp.arange(SIDE + 2 * half_width)
    narrow = jnp.arange(SIDE)
    col_band = tap_band(col_taps, wide_index[:, None] - narrow[None, :])
    filtered = jnp.einsum(
        "bpyc,bcx->bpyx", window, col_band, preferred_element_type=jnp.float32
    ).astype(jnp.bfloat16)
    padded = with_halo(filtered, (("raft", 2),), half_width)
    row_band = tap_band(row_taps, wide_index[None, :] - narrow[:, None])
    stacked = jnp.einsum("byr,bprx->pyx", row_band, padded, preferred_element_type=jnp.float32)
    summed, weight_total = (
        lax.psum_scatter(stacked, "visit", scatter_dimension=0, tiled=True),
        lax.psum_scatter(weight_sum, "visit", scatter_dimension=0, tiled=True),
    )
    coadd_image = summed / (1.0 + weight_total)[:, None, None]
    return coadd_image[None]


def filter_kernel(final, lines, mix_ref, got_ref, col_ref, row_ref, *rest):
    if final:
        before_ref, out_ref, planes, strip, filtered, total = rest
    else:
        weight_ref, out_ref, after_ref, planes, strip, filtered, total = rest
    step = pl.program_id(0)
    count = GROUP * PATCH_DEV
    blocks = PATCH_DEV + 1

    def make_planes(pair, carry):
        start = pl.multiple_of(pair * 2 * SIDE, 2 * SIDE)
        both = jnp.dot(
            mix_ref[...], got_ref[:, pl.ds(start, 2 * SIDE)], preferred_element_type=jnp.float32
        )
        row = pair * 2 * (count + 1)
        planes[pl.ds(row, count), :] = both[:, :SIDE]
        planes[pl.ds(row + count + 1, count), :] = both[:, SIDE:]
        return carry

    lax.fori_loop(0, lines // 2, make_planes, 0, unroll=4)

    @pl.when(step == 0)
    def _():
        strip[:lines, :SIDE] = jnp.zeros((lines, SIDE), jnp.bfloat16)
        strip[PATCH_DEV * lines :, SIDE:] = jnp.zeros((lines, SIDE), jnp.bfloat16)

    def filter_columns(basis, carry):
        for place in range(PATCH_DEV):
            image = planes[pl.ds(basis * PATCH_DEV + place, lines, stride=count + 1), :]
            image = image.astype(jnp.bfloat16)
            strip[place * lines : (place + 1) * lines, SIDE:] = image
            strip[(place + 1) * lines : (place + 2) * lines, :SIDE] = image
        rows = pl.ds(pl.multiple_of(basis * lines, 16), lines)
        wide = jnp.dot(strip[...], col_ref[basis], preferred_element_type=jnp.float32)
        wide = wide.astype(jnp.bfloat16)
        for block in range(blocks):
            low = block * SIDE
            filtered[rows, low : low + SIDE] = wide[block * lines : (block + 1) * lines]
        return carry

    lax.fori_loop(0, GROUP, filter_columns, 0)

    width = 5 * SIDE
    for chunk in range(blocks // 5):
        span = slice(chunk * width, (chunk + 1) * width)
        part = jnp.dot(row_ref[0], filtered[:, span], preferred_element_type=jnp.float32)
        start = before_ref[:, span] if final else 0.0
        total[:, span] = part + jnp.where(step == 0, start, total[:, span])

    @pl.when(step == NB // GROUP - 1)
    def _():
        ready = out_ref.shape[1]
        for place in range(PATCH_DEV):
            low = place * SIDE + SIDE // 2
            image = total[:ready, low : low + SIDE]
            if final:
                out_ref[place] = image.astype(jnp.bfloat16)
            else:
                out_ref[place, :16] = (image[:16] + weight_ref[place]).astype(jnp.bfloat16)
                out_ref[place, 16:] = image[16:].astype(jnp.bfloat16)
        if not final:
            after_ref[...] = total[ready:, :]


def place_kernel(placing_ref, tiles_ref, terms_ref, out_ref):
    out_ref[...] = jnp.dot(
        placing_ref[...], tiles_ref[...], preferred_element_type=jnp.float32
    ).astype(jnp.bfloat16)

    @pl.when(pl.program_id(0) == pl.num_programs(0) - 1)
    def _():
        last = out_ref.shape[1] - SIDE
        out_ref[:, last:] = jnp.dot(
            placing_ref[...], terms_ref[...], preferred_element_type=jnp.float32
        ).astype(jnp.bfloat16)


def place_first(placing, tiles, terms):
    slots, tile_count = placing.shape
    steps = 9
    width = (FIRST + 1) * SIDE // steps
    return pl.pallas_call(
        place_kernel,
        grid=(steps,),
        out_shape=jax.ShapeDtypeStruct((slots, steps * width), jnp.bfloat16),
        in_specs=[
            pl.BlockSpec((slots, tile_count), lambda s: (0, 0)),
            pl.BlockSpec((tile_count, width), lambda s: (0, s)),
            pl.BlockSpec((tile_count, SIDE), lambda s: (0, 0)),
        ],
        out_specs=pl.BlockSpec((slots, width), lambda s: (0, s)),
        compiler_params=pltpu.CompilerParams(vmem_limit_bytes=56 * 1024 * 1024),
        cost_estimate=pl.CostEstimate(
            flops=2 * slots * tile_count * steps * width,
            bytes_accessed=2 * (slots + tile_count) * steps * width,
            transcendentals=0,
        ),
    )(placing, tiles, terms)


def filter_tiles(lines, mix, got, col_band, row_band, before=None, weight=None):
    slots, pixels = got.shape
    steps = NB // GROUP
    count = GROUP * PATCH_DEV
    blocks = PATCH_DEV + 1
    final = before is not None
    rows = row_band.shape[1]
    args = [mix, got, col_band, row_band]
    in_specs = [
        pl.BlockSpec((count, slots), lambda s: (s, 0)),
        pl.BlockSpec((slots, pixels), lambda s: (0, 0)),
        pl.BlockSpec((GROUP, 2 * SIDE, SIDE), lambda s: (s, 0, 0)),
        pl.BlockSpec((1, rows, GROUP * lines), lambda s: (s, 0, 0)),
    ]
    later = pl.BlockSpec((OUT_ROWS - FIRST, blocks * SIDE), lambda s: (0, 0))
    scratch = [
        pltpu.VMEM((lines * (count + 1) + 16, SIDE), jnp.float32),
        pltpu.VMEM((blocks * lines, 2 * SIDE), jnp.bfloat16),
        pltpu.VMEM((GROUP * lines, blocks * SIDE), jnp.bfloat16),
        pltpu.VMEM((rows, blocks * SIDE), jnp.float32),
    ]
    ready = rows if final else FIRST
    out_shape = [jax.ShapeDtypeStruct((PATCH_DEV, ready, SIDE), jnp.bfloat16)]
    out_specs = [pl.BlockSpec((PATCH_DEV, ready, SIDE), lambda s: (0, 0, 0))]
    if final:
        args += [before]
        in_specs += [later]
    else:
        args += [weight]
        in_specs += [pl.BlockSpec((PATCH_DEV, 16, SIDE), lambda s: (0, 0, 0))]
        out_shape += [jax.ShapeDtypeStruct((OUT_ROWS - FIRST, blocks * SIDE), jnp.float32)]
        out_specs += [later]
    return pl.pallas_call(
        functools.partial(filter_kernel, final, lines),
        grid=(steps,),
        out_shape=out_shape,
        in_specs=in_specs,
        out_specs=out_specs,
        scratch_shapes=scratch,
        compiler_params=pltpu.CompilerParams(vmem_limit_bytes=56 * 1024 * 1024),
        cost_estimate=pl.CostEstimate(
            flops=200_000_000 * lines, bytes_accessed=100_000 * lines, transcendentals=0
        ),
    )(*args)


def plane_body(visits, depth, cores, tiles, weights, coef, owner, patch, row_taps, col_taps):
    tile_count = tiles.shape[0]
    owners = depth * cores
    capacity = 2 * tile_count // owners
    every = ("visit", "z", "core")
    owner_ids = owner[:, 0]
    share = PATCH_DEV // visits
    plain_weight = weights.astype(jnp.bfloat16)[:, None]
    owner_hits = (owner_ids[:, None] == jnp.arange(owners)[None, :]).astype(jnp.int32)
    slot_rank = jnp.sum(jnp.cumsum(owner_hits, axis=0) * owner_hits, axis=1) - 1
    slot_index = owner_ids * capacity + slot_rank
    placing = (jnp.arange(owners * capacity)[:, None] == slot_index[None, :]).astype(jnp.bfloat16)
    scaled = (weights[:, None] * coef).astype(jnp.bfloat16)
    patch_hits = (patch[:, None] == jnp.arange(PATCH_DEV)[None, :]).astype(jnp.bfloat16)
    blank = jnp.zeros((tile_count, SIDE - NB - PATCH_DEV - 1), jnp.bfloat16)
    terms = jnp.concatenate([scaled, patch_hits, plain_weight, blank], axis=1)

    def place(values):
        return jnp.dot(placing, values, preferred_element_type=jnp.float32).astype(jnp.bfloat16)

    def exchange(values):
        return lax.all_to_all(
            values, ("visit", "core"), split_axis=0, concat_axis=0, tiled=True
        )

    cut = FIRST * SIDE
    got_first = exchange(place_first(placing, tiles, terms))
    got_first, held = lax.optimization_barrier((got_first, place(tiles[:, cut:])))
    got_second = exchange(held)
    got_terms = got_first[:, cut:]
    by_basis = got_terms[:, :NB].T
    hits = got_terms[:, NB : NB + PATCH_DEV]
    mix = (by_basis[:, None, :] * hits.T[None, :, :]).reshape(NB * PATCH_DEV, -1)
    got_weight = got_terms[:, NB + PATCH_DEV :][:, :1].astype(jnp.float32)
    weight_sum = jnp.sum(got_weight * hits.astype(jnp.float32), axis=0)
    high = lax.reduce_precision(weight_sum, 8, 7)
    halves = jnp.stack([high, weight_sum - high], axis=1)
    weight_rows = jnp.pad(halves, ((0, 0), (0, 14)))[:, :, None]
    weight_rows = jnp.broadcast_to(weight_rows, (PATCH_DEV, 16, SIDE))

    wide_index = jnp.arange(2 * SIDE)
    narrow = jnp.arange(SIDE)
    col_band = tap_band(col_taps, wide_index[:, None] - narrow[None, :] - SIDE // 2 + HALF)
    out_index = jnp.arange(OUT_ROWS)
    row_band = tap_band(row_taps, narrow[None, :] - out_index[:, None] + TOP + HALF)
    row_band = row_band.reshape(NB // GROUP, GROUP, OUT_ROWS, SIDE).transpose(0, 2, 1, 3)
    row_first = row_band[..., :FIRST].reshape(NB // GROUP, OUT_ROWS, -1)
    row_second = row_band[:, FIRST:, :, FIRST:].reshape(NB // GROUP, OUT_ROWS - FIRST, -1)
    early, partial = filter_tiles(
        FIRST, mix, got_first, col_band, row_first, weight=weight_rows
    )
    (late,) = filter_tiles(SIDE - FIRST, mix, got_second, col_band, row_second, before=partial)

    def to_shares(values):
        parts = lax.all_to_all(values, "z", split_axis=0, concat_axis=0, tiled=True)
        return parts.reshape(depth, share, -1, SIDE).astype(jnp.float32)

    parts = to_shares(early)
    plane_weight = jnp.sum(parts[:, :, :2], axis=(0, 2))
    summed = jnp.sum(parts, axis=0).astype(jnp.bfloat16)
    summed_late = jnp.sum(to_shares(late), axis=0).astype(jnp.bfloat16)

    def to_owner(values, shift):
        pairs = []
        for v in range(visits):
            for q in range(depth):
                for c in range(cores):
                    target = v * cores + c + shift
                    if 0 <= target < owners:
                        pairs.append(((v * depth + q) * cores + c, q * owners + target))
        return lax.ppermute(values, every, pairs).astype(jnp.float32)

    head = to_owner(summed[:, TOP:], 0)
    tail = to_owner(summed_late[:, : TOP + SIDE - FIRST], 0)
    center = jnp.concatenate([head, tail], axis=1)
    lower = to_owner(summed[:, TOP - HALF : TOP], -1)
    low = TOP + SIDE - FIRST
    upper = to_owner(summed_late[:, low : low + HALF], 1)
    own_weight = to_owner(plane_weight, 0)
    rest = ((0, 0), (0, SIDE - HALF), (0, 0))
    numerator = center + jnp.pad(upper, rest)
    numerator = numerator + jnp.pad(lower, ((0, 0), (SIDE - HALF, 0), (0, 0)))
    return (numerator / (1.0 + own_weight)[:, None, :])[None]


def solution(mesh):
    visits, rafts = mesh.shape["visit"], mesh.shape["raft"]
    cores = 2
    if visits * cores == rafts and PATCH_DEV % visits == 0:
        depth = rafts // cores
        split = Mesh(mesh.devices.reshape(visits, depth, cores), ("visit", "z", "core"))
        every = ("visit", "z", "core")
        placed = (P(every, None), P(every), P(every, None), P(every, None), P(every), P(), P())
        return jax.shard_map(
            functools.partial(plane_body, visits, depth, cores),
            mesh=split,
            in_specs=placed,
            out_specs=P(("z", "core"), "visit", None, None),
            check_vma=False,
        )
    placed = (
        P(("visit", "raft"), None),
        P(("visit", "raft")),
        P(("visit", "raft"), None),
        P(("visit", "raft"), None),
        P(("visit", "raft")),
        P(),
        P(),
    )
    return jax.shard_map(
        body, mesh=mesh, in_specs=placed, out_specs=P("raft", "visit", None, None), check_vma=False
    )
```

```python
import functools

import jax
import jax.numpy as jnp
from jax import lax
from jax.experimental import pallas as pl
from jax.experimental.pallas import tpu as pltpu
from jax.sharding import Mesh, PartitionSpec as P

SIDE = 128
KERNEL = 41
NB = 27
PATCH_DEV = 24
GROUP = 9
HALF = (KERNEL - 1) // 2
TOP = 24
OUT_ROWS = 176
FIRST = 80


def with_halo(shard, sides, width):
    for axis, dim in sides:
        size, length = (lax.axis_size(axis), shard.shape[dim])
        up = [(i, (i + 1) % size) for i in range(size - 1)]
        down = [(j, i) for i, j in up]
        last = lax.slice_in_dim(shard, length - width, length, axis=dim)
        leading = lax.slice_in_dim(shard, 0, width, axis=dim)
        before = lax.ppermute(last, axis, up)
        after = lax.ppermute(leading, axis, down)
        shard = jnp.concatenate([before, shard, after], axis=dim)
    return shard


def tap_band(tap_values, offsets):
    selector = (offsets[:, :, None] == jnp.arange(tap_values.shape[1])[None, None, :]).astype(
        jnp.float32
    )
    return jnp.einsum("qrj,bj->bqr", selector, tap_values.astype(jnp.float32)).astype(jnp.bfloat16)


def body(tiles, weights, coef, owner, patch, row_taps, col_taps):
    tile_count = tiles.shape[0]
    peer_count = lax.axis_size("raft")
    capacity = max(2, 2 * tile_count // peer_count)
    half_width = (KERNEL - 1) // 2
    owner_ids = owner[:, 0]
    owner_hits = (owner_ids[:, None] == jnp.arange(peer_count)[None, :]).astype(jnp.int32)
    slot_rank = jnp.sum(jnp.cumsum(owner_hits, axis=0) * owner_hits, axis=1) - 1
    slot_index = owner_ids * capacity + slot_rank
    placing = (jnp.arange(peer_count * capacity)[:, None] == slot_index[None, :]).astype(
        jnp.bfloat16
    )
    scaled = (weights[:, None] * coef).astype(jnp.bfloat16)
    plain_weight = weights.astype(jnp.bfloat16)[:, None]
    tile_terms = jnp.concatenate([scaled, plain_weight], axis=1)
    patch_hits = (patch[:, None] == jnp.arange(PATCH_DEV)[None, :]).astype(jnp.bfloat16)
    mixing = (tile_terms[:, :, None] * patch_hits[:, None, :]).reshape(
        tile_count, (NB + 1) * PATCH_DEV
    )
    send_tiles = jnp.dot(placing, tiles, preferred_element_type=jnp.float32).astype(jnp.bfloat16)
    send_mixing = jnp.dot(placing, mixing, preferred_element_type=jnp.float32).astype(jnp.bfloat16)
    got_tiles, got_mixing = (
        lax.all_to_all(send_tiles, "raft", split_axis=0, concat_axis=0, tiled=True),
        lax.all_to_all(send_mixing, "raft", split_axis=0, concat_axis=0, tiled=True),
    )
    planes = lax.dot_general(
        got_mixing[:, : NB * PATCH_DEV],
        got_tiles,
        (((0,), (0,)), ((), ())),
        preferred_element_type=jnp.float32,
    )
    planes = planes.astype(jnp.bfloat16).reshape(NB, PATCH_DEV, SIDE, SIDE)
    weight_sum = jnp.sum(got_mixing[:, NB * PATCH_DEV :].astype(jnp.float32), axis=0)
    blank_rim = jnp.zeros((NB, 1, SIDE, half_width), jnp.bfloat16)
    left_rim = jnp.concatenate([blank_rim, planes[:, :-1, :, SIDE - half_width :]], axis=1)
    right_rim = jnp.concatenate([planes[:, 1:, :, :half_width], blank_rim], axis=1)
    window = jnp.concatenate([left_rim, planes, right_rim], axis=3)
    wide_index = jnp.arange(SIDE + 2 * half_width)
    narrow = jnp.arange(SIDE)
    col_band = tap_band(col_taps, wide_index[:, None] - narrow[None, :])
    filtered = jnp.einsum(
        "bpyc,bcx->bpyx", window, col_band, preferred_element_type=jnp.float32
    ).astype(jnp.bfloat16)
    padded = with_halo(filtered, (("raft", 2),), half_width)
    row_band = tap_band(row_taps, wide_index[None, :] - narrow[:, None])
    stacked = jnp.einsum("byr,bprx->pyx", row_band, padded, preferred_element_type=jnp.float32)
    summed, weight_total = (
        lax.psum_scatter(stacked, "visit", scatter_dimension=0, tiled=True),
        lax.psum_scatter(weight_sum, "visit", scatter_dimension=0, tiled=True),
    )
    coadd_image = summed / (1.0 + weight_total)[:, None, None]
    return coadd_image[None]


def filter_kernel(final, lines, mix_ref, got_ref, col_ref, row_ref, *rest):
    if final:
        before_ref, out_ref, planes, strip, filtered, total = rest
    else:
        weight_ref, out_ref, after_ref, planes, strip, filtered, total = rest
    step = pl.program_id(0)
    count = GROUP * PATCH_DEV
    blocks = PATCH_DEV + 1

    def make_planes(pair, carry):
        start = pl.multiple_of(pair * 2 * SIDE, 2 * SIDE)
        both = jnp.dot(
            mix_ref[...], got_ref[:, pl.ds(start, 2 * SIDE)], preferred_element_type=jnp.float32
        )
        row = pair * 2 * (count + 1)
        planes[pl.ds(row, count), :] = both[:, :SIDE]
        planes[pl.ds(row + count + 1, count), :] = both[:, SIDE:]
        return carry

    lax.fori_loop(0, lines // 2, make_planes, 0, unroll=4)

    @pl.when(step == 0)
    def _():
        strip[:lines, :SIDE] = jnp.zeros((lines, SIDE), jnp.bfloat16)
        strip[PATCH_DEV * lines :, SIDE:] = jnp.zeros((lines, SIDE), jnp.bfloat16)

    def filter_columns(basis, carry):
        for place in range(PATCH_DEV):
            image = planes[pl.ds(basis * PATCH_DEV + place, lines, stride=count + 1), :]
            image = image.astype(jnp.bfloat16)
            strip[place * lines : (place + 1) * lines, SIDE:] = image
            strip[(place + 1) * lines : (place + 2) * lines, :SIDE] = image
        rows = pl.ds(pl.multiple_of(basis * lines, 16), lines)
        wide = jnp.dot(strip[...], col_ref[basis], preferred_element_type=jnp.float32)
        wide = wide.astype(jnp.bfloat16)
        for block in range(blocks):
            low = block * SIDE
            filtered[rows, low : low + SIDE] = wide[block * lines : (block + 1) * lines]
        return carry

    lax.fori_loop(0, GROUP, filter_columns, 0)

    width = 5 * SIDE
    for chunk in range(blocks // 5):
        span = slice(chunk * width, (chunk + 1) * width)
        part = jnp.dot(row_ref[0], filtered[:, span], preferred_element_type=jnp.float32)
        start = before_ref[:, span] if final else 0.0
        total[:, span] = part + jnp.where(step == 0, start, total[:, span])

    @pl.when(step == NB // GROUP - 1)
    def _():
        ready = out_ref.shape[1]
        for place in range(PATCH_DEV):
            low = place * SIDE + SIDE // 2
            image = total[:ready, low : low + SIDE]
            if final:
                out_ref[place] = image.astype(jnp.bfloat16)
            else:
                out_ref[place, :16] = (image[:16] + weight_ref[place]).astype(jnp.bfloat16)
                out_ref[place, 16:] = image[16:].astype(jnp.bfloat16)
        if not final:
            after_ref[...] = total[ready:, :]


def place_kernel(placing_ref, tiles_ref, terms_ref, out_ref):
    out_ref[...] = jnp.dot(
        placing_ref[...], tiles_ref[...], preferred_element_type=jnp.float32
    ).astype(jnp.bfloat16)

    @pl.when(pl.program_id(0) == pl.num_programs(0) - 1)
    def _():
        last = out_ref.shape[1] - SIDE
        out_ref[:, last:] = jnp.dot(
            placing_ref[...], terms_ref[...], preferred_element_type=jnp.float32
        ).astype(jnp.bfloat16)


def place_first(placing, tiles, terms):
    slots, tile_count = placing.shape
    steps = 3
    width = (FIRST + 1) * SIDE // steps
    return pl.pallas_call(
        place_kernel,
        grid=(steps,),
        out_shape=jax.ShapeDtypeStruct((slots, steps * width), jnp.bfloat16),
        in_specs=[
            pl.BlockSpec((slots, tile_count), lambda s: (0, 0)),
            pl.BlockSpec((tile_count, width), lambda s: (0, s)),
            pl.BlockSpec((tile_count, SIDE), lambda s: (0, 0)),
        ],
        out_specs=pl.BlockSpec((slots, width), lambda s: (0, s)),
        compiler_params=pltpu.CompilerParams(vmem_limit_bytes=56 * 1024 * 1024),
        cost_estimate=pl.CostEstimate(
            flops=2 * slots * tile_count * steps * width,
            bytes_accessed=2 * (slots + tile_count) * steps * width,
            transcendentals=0,
        ),
    )(placing, tiles, terms)


def filter_tiles(lines, mix, got, col_band, row_band, before=None, weight=None):
    slots, pixels = got.shape
    steps = NB // GROUP
    count = GROUP * PATCH_DEV
    blocks = PATCH_DEV + 1
    final = before is not None
    rows = row_band.shape[1]
    args = [mix, got, col_band, row_band]
    in_specs = [
        pl.BlockSpec((count, slots), lambda s: (s, 0)),
        pl.BlockSpec((slots, pixels), lambda s: (0, 0)),
        pl.BlockSpec((GROUP, 2 * SIDE, SIDE), lambda s: (s, 0, 0)),
        pl.BlockSpec((1, rows, GROUP * lines), lambda s: (s, 0, 0)),
    ]
    later = pl.BlockSpec((OUT_ROWS - FIRST, blocks * SIDE), lambda s: (0, 0))
    scratch = [
        pltpu.VMEM((lines * (count + 1) + 16, SIDE), jnp.float32),
        pltpu.VMEM((blocks * lines, 2 * SIDE), jnp.bfloat16),
        pltpu.VMEM((GROUP * lines, blocks * SIDE), jnp.bfloat16),
        pltpu.VMEM((rows, blocks * SIDE), jnp.float32),
    ]
    ready = rows if final else FIRST
    out_shape = [jax.ShapeDtypeStruct((PATCH_DEV, ready, SIDE), jnp.bfloat16)]
    out_specs = [pl.BlockSpec((PATCH_DEV, ready, SIDE), lambda s: (0, 0, 0))]
    if final:
        args += [before]
        in_specs += [later]
    else:
        args += [weight]
        in_specs += [pl.BlockSpec((PATCH_DEV, 16, SIDE), lambda s: (0, 0, 0))]
        out_shape += [jax.ShapeDtypeStruct((OUT_ROWS - FIRST, blocks * SIDE), jnp.float32)]
        out_specs += [later]
    return pl.pallas_call(
        functools.partial(filter_kernel, final, lines),
        grid=(steps,),
        out_shape=out_shape,
        in_specs=in_specs,
        out_specs=out_specs,
        scratch_shapes=scratch,
        compiler_params=pltpu.CompilerParams(vmem_limit_bytes=56 * 1024 * 1024),
        cost_estimate=pl.CostEstimate(
            flops=200_000_000 * lines, bytes_accessed=100_000 * lines, transcendentals=0
        ),
    )(*args)


def plane_body(visits, depth, cores, tiles, weights, coef, owner, patch, row_taps, col_taps):
    tile_count = tiles.shape[0]
    owners = depth * cores
    capacity = 2 * tile_count // owners
    every = ("visit", "z", "core")
    owner_ids = owner[:, 0]
    share = PATCH_DEV // visits
    plain_weight = weights.astype(jnp.bfloat16)[:, None]
    owner_hits = (owner_ids[:, None] == jnp.arange(owners)[None, :]).astype(jnp.int32)
    slot_rank = jnp.sum(jnp.cumsum(owner_hits, axis=0) * owner_hits, axis=1) - 1
    slot_index = owner_ids * capacity + slot_rank
    placing = (jnp.arange(owners * capacity)[:, None] == slot_index[None, :]).astype(jnp.bfloat16)
    scaled = (weights[:, None] * coef).astype(jnp.bfloat16)
    patch_hits = (patch[:, None] == jnp.arange(PATCH_DEV)[None, :]).astype(jnp.bfloat16)
    blank = jnp.zeros((tile_count, SIDE - NB - PATCH_DEV - 1), jnp.bfloat16)
    terms = jnp.concatenate([scaled, patch_hits, plain_weight, blank], axis=1)

    def place(values):
        return jnp.dot(placing, values, preferred_element_type=jnp.float32).astype(jnp.bfloat16)

    def exchange(values):
        return lax.all_to_all(
            values, ("visit", "core"), split_axis=0, concat_axis=0, tiled=True
        )

    cut = FIRST * SIDE
    got_first = exchange(place_first(placing, tiles, terms))
    got_first, held = lax.optimization_barrier((got_first, place(tiles[:, cut:])))
    got_second = exchange(held)
    got_terms = got_first[:, cut:]
    by_basis = got_terms[:, :NB].T
    hits = got_terms[:, NB : NB + PATCH_DEV]
    mix = (by_basis[:, None, :] * hits.T[None, :, :]).reshape(NB * PATCH_DEV, -1)
    got_weight = got_terms[:, NB + PATCH_DEV :][:, :1].astype(jnp.float32)
    weight_sum = jnp.sum(got_weight * hits.astype(jnp.float32), axis=0)
    high = lax.reduce_precision(weight_sum, 8, 7)
    halves = jnp.stack([high, weight_sum - high], axis=1)
    weight_rows = jnp.pad(halves, ((0, 0), (0, 14)))[:, :, None]
    weight_rows = jnp.broadcast_to(weight_rows, (PATCH_DEV, 16, SIDE))

    wide_index = jnp.arange(2 * SIDE)
    narrow = jnp.arange(SIDE)
    col_band = tap_band(col_taps, wide_index[:, None] - narrow[None, :] - SIDE // 2 + HALF)
    out_index = jnp.arange(OUT_ROWS)
    row_band = tap_band(row_taps, narrow[None, :] - out_index[:, None] + TOP + HALF)
    row_band = row_band.reshape(NB // GROUP, GROUP, OUT_ROWS, SIDE).transpose(0, 2, 1, 3)
    row_first = row_band[..., :FIRST].reshape(NB // GROUP, OUT_ROWS, -1)
    row_second = row_band[:, FIRST:, :, FIRST:].reshape(NB // GROUP, OUT_ROWS - FIRST, -1)
    early, partial = filter_tiles(
        FIRST, mix, got_first, col_band, row_first, weight=weight_rows
    )
    (late,) = filter_tiles(SIDE - FIRST, mix, got_second, col_band, row_second, before=partial)

    def to_shares(values):
        parts = lax.all_to_all(values, "z", split_axis=0, concat_axis=0, tiled=True)
        return parts.reshape(depth, share, -1, SIDE).astype(jnp.float32)

    parts = to_shares(early)
    plane_weight = jnp.sum(parts[:, :, :2], axis=(0, 2))
    summed = jnp.sum(parts, axis=0).astype(jnp.bfloat16)
    summed_late = jnp.sum(to_shares(late), axis=0).astype(jnp.bfloat16)

    def to_owner(values, shift):
        pairs = []
        for v in range(visits):
            for q in range(depth):
                for c in range(cores):
                    target = v * cores + c + shift
                    if 0 <= target < owners:
                        pairs.append(((v * depth + q) * cores + c, q * owners + target))
        return lax.ppermute(values, every, pairs).astype(jnp.float32)

    head = to_owner(summed[:, TOP:], 0)
    tail = to_owner(summed_late[:, : TOP + SIDE - FIRST], 0)
    center = jnp.concatenate([head, tail], axis=1)
    lower = to_owner(summed[:, TOP - HALF : TOP], -1)
    low = TOP + SIDE - FIRST
    upper = to_owner(summed_late[:, low : low + HALF], 1)
    own_weight = to_owner(plane_weight, 0)
    rest = ((0, 0), (0, SIDE - HALF), (0, 0))
    numerator = center + jnp.pad(upper, rest)
    numerator = numerator + jnp.pad(lower, ((0, 0), (SIDE - HALF, 0), (0, 0)))
    return (numerator / (1.0 + own_weight)[:, None, :])[None]


def solution(mesh):
    visits, rafts = mesh.shape["visit"], mesh.shape["raft"]
    cores = 2
    if visits * cores == rafts and PATCH_DEV % visits == 0:
        depth = rafts // cores
        split = Mesh(mesh.devices.reshape(visits, depth, cores), ("visit", "z", "core"))
        every = ("visit", "z", "core")
        placed = (P(every, None), P(every), P(every, None), P(every, None), P(every), P(), P())
        return jax.shard_map(
            functools.partial(plane_body, visits, depth, cores),
            mesh=split,
            in_specs=placed,
            out_specs=P(("z", "core"), "visit", None, None),
            check_vma=False,
        )
    placed = (
        P(("visit", "raft"), None),
        P(("visit", "raft")),
        P(("visit", "raft"), None),
        P(("visit", "raft"), None),
        P(("visit", "raft")),
        P(),
        P(),
    )
    return jax.shard_map(
        body, mesh=mesh, in_specs=placed, out_specs=P("raft", "visit", None, None), check_vma=False
    )
```
